1024 devices in a mesh: row: 16 (over y, x_lo), col: 64 (over x_hi, z, core).
Axes of the slice: x: 8 (x_hi: 4, x_lo: 2; x = x_hi * 2 + x_lo), y: 8, z: 8, core: 2. Of those that a mesh axis runs over, the one named last changes fastest.
Arguments:
- features: bfloat16 [131072, 128], P(('col', 'row')), may hold values from -6 to 6
- tile_row: int32 [16, 64, 96], P('row', 'col'), may hold values from 0 to 63, as said below
- tile_col: int32 [16, 64, 96], P('row', 'col'), may hold values from 0 to 15
- tile_count: int32 [16, 64], P('row', 'col'), may hold values from 24 to 96, as said below
- tile_vals: bfloat16 [16, 64, 96, 128, 128], P('row', 'col'), may hold values from -0.0546875 to 0.0546875
- weight: bfloat16 [128, 128], replicated, may hold values from -0.5 to 0.5
- cotangent: bfloat16 [131072, 128], P(('row', 'col')), may hold values from -6 to 6
Outputs:
- layer_out: bfloat16 [131072, 128], P(('row', 'col'))
- weight_grad: float32 [128, 128], replicated
The draws below stay inside these ranges and needn't reach their ends.
Inputs may be any that keep to these rules, and one draw needn't show every extreme that they name: Within one block the pairs (tile_row, tile_col) of all 96 slots are distinct. `tile_count`: at least 24; some block has all 96 slots live.
All inputs are finite; a program needn't handle non-finite values.
Results may differ from the reference program's by a relative error of at most 0.0053.
Values may be sent and summed in bfloat16 or wider, within the bound.
A program may use at most 64 MiB of HBM per device.

```python
import jax
import jax.numpy as jnp
from jax import lax

F = 128
TILE = 128
BLOCK_ROWS = 16
BLOCK_COLS = 64
NODES = 131072
TR = 64
TC = 16
MAXT = 96


def tile_slots(key):
    slot_total = TR * TC
    scores = jax.random.randint(key, (BLOCK_ROWS, BLOCK_COLS, slot_total), 0, 65536)
    distinct = scores * slot_total + jnp.arange(slot_total, dtype=jnp.int32)
    ordering = jnp.argsort(distinct, axis=-1)
    return ordering[..., :MAXT].astype(jnp.int32)


def draw_tile_row(key, part):
    chosen = tile_slots(key)
    return (chosen // TC).astype(jnp.int32)


def draw_tile_col(key, part):
    chosen = tile_slots(key)
    return (chosen % TC).astype(jnp.int32)


def draw_tile_count(key, part):
    key = jax.random.fold_in(key, 3)
    first_key, second_key = jax.random.split(key)
    lowest = max(MAXT // 4, 1)
    counts = jax.random.randint(first_key, (BLOCK_ROWS, BLOCK_COLS), lowest, MAXT + 1)
    fullest = jax.random.randint(second_key, (), 0, BLOCK_ROWS * BLOCK_COLS)
    flat_index = jnp.arange(BLOCK_ROWS * BLOCK_COLS, dtype=jnp.int32).reshape(BLOCK_ROWS, BLOCK_COLS)
    return jnp.where(flat_index == fullest, MAXT, counts).astype(jnp.int32)


def shard_levels(rng, dims, shards, smallest, high):
    factor_of, own = 1.0, jax.random.fold_in(rng, 6)
    for position, parts in shards:
        draws = jnp.exp(jax.random.uniform(jax.random.fold_in(own, position), (parts,), jnp.float32, smallest / len(shards), high / len(shards)))
        factor_of = factor_of * jnp.repeat(draws, dims[position] // parts).reshape([-1 if axis == position else 1 for axis in range(len(dims))])
    return factor_of


def gaussian(stream_key, shape, width, limit, shards=(), held_as=jnp.bfloat16):
    values = jax.random.normal(stream_key, shape, jnp.float32) * width
    if len(shards) > 0:
        values = shard_levels(stream_key, shape, shards, -0.22, 0.18) * values
    return jnp.clip(values, min=-limit, max=limit).astype(held_as)


def setup_inputs(seed: int = 0) -> dict:
    seeds = jax.random.split(jax.random.key(seed), 8)
    return {
        "features": gaussian(seeds[0], (NODES, F), 1.0, 6.0, ((0, 1024),)),
        "tile_row": draw_tile_row(jax.random.fold_in(seeds[7], 71), 0),
        "tile_col": draw_tile_col(jax.random.fold_in(seeds[7], 71), 0),
        "tile_count": draw_tile_count(jax.random.fold_in(seeds[7], 71), 0),
        "tile_vals": gaussian(seeds[4], (BLOCK_ROWS, BLOCK_COLS, MAXT, TILE, TILE), (TILE * MAXT * BLOCK_COLS // TR) ** -0.5, 0.0546875, ((0, 16), (1, 64))),
        "weight": gaussian(seeds[5], (F, F), F ** -0.5, 0.5),
        "cotangent": gaussian(seeds[6], (NODES, F), 1.0, 6.0, ((0, 1024),)),
    }


def reference(features, tile_row, tile_col, tile_count, tile_vals, weight, cotangent):
    band_cols = TC * TILE
    band_rows = TR * TILE

    def row_band(block_row):
        def add_block(running, block_col):
            source = lax.dynamic_slice_in_dim(features, (block_col * band_cols).astype(jnp.int32), band_cols, 0)
            source = source.reshape(TC, TILE, F)
            picked = source[tile_col[block_row, block_col]].astype(jnp.float32)
            entries = tile_vals[block_row, block_col].astype(jnp.float32)
            active = (jnp.arange(MAXT) < tile_count[block_row, block_col]).astype(jnp.float32)
            products = jnp.einsum("tab,tbf->taf", entries, picked) * active[:, None, None]
            added = jax.ops.segment_sum(products, tile_row[block_row, block_col], num_segments=TR)
            return running + added, None

        running, _ = lax.scan(add_block, jnp.zeros((TR, TILE, F), jnp.float32), jnp.arange(BLOCK_COLS, dtype=jnp.int32))
        return running.reshape(band_rows, F)

    aggregated = lax.map(row_band, jnp.arange(BLOCK_ROWS, dtype=jnp.int32)).reshape(NODES, F).astype(jnp.bfloat16)
    pre = jnp.dot(aggregated, weight, preferred_element_type=jnp.float32)
    layer_out = jax.nn.silu(pre).astype(jnp.bfloat16)
    sigmoid_pre = jax.nn.sigmoid(pre)
    derivative = sigmoid_pre * (1.0 + pre * (1.0 - sigmoid_pre))
    grad_pre = (cotangent.astype(jnp.float32) * derivative).astype(jnp.bfloat16)
    weight_grad = jnp.dot(aggregated.T, grad_pre, preferred_element_type=jnp.float32)
    return layer_out, weight_grad
```

```python
import jax
import jax.numpy as jnp
from jax import lax
from jax.experimental import pallas as pl
from jax.experimental.pallas import tpu as pltpu
from jax.sharding import PartitionSpec as P

NY, NXL, NXH, NZ, NC = 8, 2, 4, 8, 2
NX = NXH * NXL
S = 128
SLOTS = 96
ROWS = 64
COLS = 16
FAR_FIRST = (4, 3, 5, 2, 6, 1, 7)
NEAR_FIRST = (1, 7, 2, 6, 3, 5, 4)
X_OFF = (2, 1, 3, 0)
PIECES = ((0, 24), (24, 24), (48, 16))
BF, F32, I32 = jnp.bfloat16, jnp.float32, jnp.int32


def span_right(k):
    return 4 if k % 2 == 0 else 3


def span_left(k):
    return 3 if k % 2 == 0 else 4


def wrap(value, size):
    return lax.rem(value + size, size)


def kernel(
    feat_ref, row_ref, col_ref, count_ref, vals_ref, weight_ref, cot_ref,
    out_ref, grad_ref,
    vals, gath, prefix, meta_v, meta_s, core_out, core_in, pair, z_out, z_in,
    x_out, x_in, part, half, half_in, stage_out, stage_in, full_in,
    vals_sem, meta_sem, g_send, g_recv, c_send, c_recv, z_send, z_recv,
    x_send, x_recv, w_send, w_recv, e_send, e_recv,
):
    row, col = lax.axis_index("row"), lax.axis_index("col")
    y, xl = lax.div(row, NXL), lax.rem(row, NXL)
    xh, z, c = lax.div(col, NZ * NC), lax.rem(lax.div(col, NC), NZ), lax.rem(col, NC)
    x = xh * NXL + xl

    def device(y=y, x=x, z=z, c=c):
        return {
            "row": y * NXL + lax.rem(x, NXL),
            "col": lax.div(x, NXL) * (NZ * NC) + z * NC + c,
        }

    def send(src, dst, send_sem, recv_sem, to):
        copy = pltpu.make_async_remote_copy(
            src_ref=src, dst_ref=dst, send_sem=send_sem, recv_sem=recv_sem,
            device_id=to, device_id_type=pl.DeviceIdType.MESH,
        )
        copy.start()
        return copy

    barrier = pltpu.get_barrier_semaphore()
    peers = [device(c=1 - c)]
    for k in FAR_FIRST:
        peers += [device(y=wrap(y + k, NY)), device(x=wrap(x + k, NX)), device(z=wrap(z + k, NZ))]
    for peer in peers:
        pl.semaphore_signal(barrier, inc=1, device_id=peer, device_id_type=pl.DeviceIdType.MESH)

    load = pltpu.make_async_copy(vals_ref.at[0, 0], vals, vals_sem)
    load.start()

    lane = lax.broadcasted_iota(I32, (SLOTS, SLOTS), 1)
    sub = lax.broadcasted_iota(I32, (SLOTS, SLOTS), 0)
    lane1 = lax.broadcasted_iota(I32, (1, SLOTS), 1)
    live = lane1 < count_ref[...]
    trow = jnp.where(live, row_ref[0], ROWS)
    tcol = jnp.where(live, col_ref[0], 0)
    trow_b = jnp.broadcast_to(trow, (SLOTS, SLOTS))
    diagonal = lane == sub
    trow_c = jnp.sum(jnp.where(diagonal, trow_b, 0), axis=1, keepdims=True)
    tcol_c = jnp.sum(jnp.where(diagonal, jnp.broadcast_to(tcol, (SLOTS, SLOTS)), 0), axis=1, keepdims=True)
    before = (trow_b < trow_c) | ((trow_b == trow_c) & (lane < sub))
    rank_c = jnp.sum(jnp.where(before, 1, 0), axis=1, keepdims=True)
    same_c = jnp.max(jnp.where((trow_b == trow_c) & (lane < sub), 1, 0), axis=1, keepdims=True)
    place = rank_c == lane
    slot_s = jnp.sum(jnp.where(place, sub, 0), axis=0, keepdims=True)
    col_s = jnp.sum(jnp.where(place, jnp.broadcast_to(tcol_c, (SLOTS, SLOTS)), 0), axis=0, keepdims=True)
    same_s = jnp.sum(jnp.where(place, jnp.broadcast_to(same_c, (SLOTS, SLOTS)), 0), axis=0, keepdims=True)
    upto = jnp.sum(jnp.where(trow_c <= lane, 1, 0), axis=0, keepdims=True)
    held = jnp.sum(jnp.where(trow_c == lane, 1, 0), axis=0, keepdims=True)
    end_s = jnp.where(held > 0, upto - 1, SLOTS)
    meta_v[...] = jnp.zeros_like(meta_v)
    meta_v[0:1, :SLOTS] = slot_s
    meta_v[1:2, :SLOTS] = col_s
    meta_v[2:3, :SLOTS] = same_s
    meta_v[3:4, :SLOTS] = end_s
    to_scalars = pltpu.make_async_copy(meta_v, meta_s, meta_sem)
    to_scalars.start()

    gath[row] = feat_ref[...]
    prefix[SLOTS] = jnp.zeros((S, S), F32)

    pl.semaphore_wait(barrier, len(peers))

    sent = []
    partner = device(x=xh * NXL + 1 - xl)
    along = {}
    for k in FAR_FIRST:
        along[k] = send(feat_ref, gath.at[row], g_send.at[k], g_recv.at[k], device(y=wrap(y + k, NY)))
    across = [send(feat_ref, gath.at[row], g_send.at[8], g_recv.at[8], partner)]
    for k in NEAR_FIRST:
        along[k].wait_recv()
        block = wrap(y - k, NY) * NXL + xl
        across.append(send(gath.at[block], gath.at[block], g_send.at[8 + k], g_recv.at[8 + k], partner))
    to_scalars.wait()
    load.wait()
    for copy in across:
        copy.wait_recv()
    sent += list(along.values()) + across

    def group(g, running):
        first = g * 8
        for u in range(8):
            s = first + u
            product = jnp.dot(vals[meta_s[0, s]], gath[meta_s[1, s]], preferred_element_type=F32)
            running = running * meta_s[2, s].astype(F32) + product
            prefix[s] = running
        return running

    lax.fori_loop(0, SLOTS // 8, group, jnp.zeros((S, S), F32))

    def tile_row(dz, k, core):
        return wrap(xh + X_OFF[k], NXH) * (NZ * NC) + wrap(z + dz, NZ) * NC + core

    swaps = {}
    other = device(c=1 - c)
    for dz in FAR_FIRST + (0,):
        for k in range(NXH):
            core_out[dz, k] = prefix[meta_s[3, tile_row(dz, k, 1 - c)]].astype(BF)
        swaps[dz] = send(core_out.at[dz], core_in.at[dz], c_send.at[dz], c_recv.at[dz], other)
    ready = set()

    def pair_sum(dz):
        if dz not in ready:
            ready.add(dz)
            swaps[dz].wait_recv()
            for k in range(NXH):
                pair[dz, k] = core_in[dz, k].astype(F32) + prefix[meta_s[3, tile_row(dz, k, c)]]

    right, left = device(z=wrap(z + 1, NZ)), device(z=wrap(z - 1, NZ))
    rings = {}
    for step in range(1, 5):
        for k in range(NXH):
            for way, span, sign, to in ((0, span_right(k), 1, right), (1, span_left(k), -1, left)):
                at = step - (4 - span)
                if at < 1:
                    continue
                dz = (sign * (span - at + 1)) % NZ
                pair_sum(dz)
                total = pair[dz, k]
                if at > 1:
                    rings[way, k, step - 1].wait_recv()
                    total = total + z_in[way, k, step - 2].astype(F32)
                z_out[way, k, step - 1] = total.astype(BF)
                rings[way, k, step] = send(
                    z_out.at[way, k, step - 1], z_in.at[way, k, step - 1],
                    z_send.at[way, k, step - 1], z_recv.at[way, k, step - 1], to,
                )
    sent += list(swaps.values())

    pair_sum(0)
    hops = []
    for k in range(NXH):
        rings[0, k, 4].wait_recv()
        rings[1, k, 4].wait_recv()
        total = pair[0, k] + z_in[0, k, 3].astype(F32) + z_in[1, k, 3].astype(F32)
        if X_OFF[k]:
            x_out[k] = total.astype(BF)
            to = device(x=wrap(xh + X_OFF[k], NXH) * NXL + xl)
            hops.append(send(x_out.at[k], x_in.at[k], x_send.at[k], x_recv.at[k], to))
    for k, copy in enumerate(hops):
        copy.wait_recv()
        total = total + x_in[k].astype(F32)
    sent += list(rings.values()) + hops

    aggregated = total.astype(BF)
    pre = jnp.dot(aggregated, weight_ref[...], preferred_element_type=F32)
    sigmoid_pre = jax.nn.sigmoid(pre)
    out_ref[...] = (pre * sigmoid_pre).astype(BF)
    derivative = sigmoid_pre * (1.0 + pre * (1.0 - sigmoid_pre))
    grad_pre = (cot_ref[...].astype(F32) * derivative).astype(BF)
    part[...] = lax.dot_general(aggregated, grad_pre, (((0,), (0,)), ((), ())), preferred_element_type=F32)

    mine = pl.ds(pl.multiple_of(c * (S // 2), S // 2), S // 2)
    theirs = pl.ds(pl.multiple_of((1 - c) * (S // 2), S // 2), S // 2)
    swap = send(part.at[theirs], half_in, e_send.at[0], e_recv.at[0], other)
    swap.wait_recv()
    half[...] = part[mine] + half_in[...]
    sent.append(swap)
    axes = (
        (z, lambda k: device(z=wrap(z + k, NZ))),
        (x, lambda k: device(x=wrap(x + k, NX))),
        (y, lambda k: device(y=wrap(y + k, NY))),
    )
    for stage in range(3):
        copies = []
        for p, (start, size) in enumerate(PIECES):
            stage_out[stage, pl.ds(start, size)] = half[pl.ds(start, size)]
        for k in FAR_FIRST:
            for p, (start, size) in enumerate(PIECES):
                place_on, to = axes[(stage + p) % 3]
                rows = pl.ds(start, size)
                copies.append(send(
                    stage_out.at[stage, rows], stage_in.at[stage, place_on, rows],
                    w_send.at[stage, p, k], w_recv.at[stage, p, k], to(k),
                ))
        for p, (start, size) in enumerate(PIECES):
            rows = pl.ds(start, size)
            stage_in[stage, axes[(stage + p) % 3][0], rows] = half[rows]
        for copy in copies:
            copy.wait_recv()
        total = stage_in[stage, 0]
        for n in range(1, 8):
            total = total + stage_in[stage, n]
        half[...] = total
        sent += copies
    swap = send(half, full_in, e_send.at[1], e_recv.at[1], other)
    grad_ref[mine] = half[...]
    swap.wait_recv()
    grad_ref[theirs] = full_in[...]
    sent.append(swap)
    for copy in sent:
        copy.wait_send()


def on_device(features, tile_row, tile_col, tile_count, tile_vals, weight, cotangent):
    vmem = pl.BlockSpec(memory_space=pltpu.VMEM)
    dma = pltpu.SemaphoreType.DMA
    return pl.pallas_call(
        kernel,
        out_shape=(jax.ShapeDtypeStruct((S, S), BF), jax.ShapeDtypeStruct((S, S), F32)),
        in_specs=[vmem, vmem, vmem, vmem, pl.BlockSpec(memory_space=pl.ANY), vmem, vmem],
        out_specs=(vmem, vmem),
        scratch_shapes=[
            pltpu.VMEM((SLOTS, S, S), BF),
            pltpu.VMEM((COLS, S, S), BF),
            pltpu.VMEM((SLOTS + 1, S, S), F32),
            pltpu.VMEM((8, S), I32),
            pltpu.SMEM((8, S), I32),
            pltpu.VMEM((NZ, NXH, S, S), BF),
            pltpu.VMEM((NZ, NXH, S, S), BF),
            pltpu.VMEM((NZ, NXH, S, S), F32),
            pltpu.VMEM((2, NXH, 4, S, S), BF),
            pltpu.VMEM((2, NXH, 4, S, S), BF),
            pltpu.VMEM((3, S, S), BF),
            pltpu.VMEM((3, S, S), BF),
            pltpu.VMEM((S, S), F32),
            pltpu.VMEM((S // 2, S), F32),
            pltpu.VMEM((S // 2, S), F32),
            pltpu.VMEM((3, S // 2, S), F32),
            pltpu.VMEM((3, 8, S // 2, S), F32),
            pltpu.VMEM((S // 2, S), F32),
            dma, dma,
            dma((16,)), dma((16,)),
            dma((NZ,)), dma((NZ,)),
            dma((2, NXH, 4)), dma((2, NXH, 4)),
            dma((3,)), dma((3,)),
            dma((3, 3, 8)), dma((3, 3, 8)),
            dma((2,)), dma((2,)),
        ],
        compiler_params=pltpu.CompilerParams(
            collective_id=0, has_side_effects=True, vmem_limit_bytes=40 * 2**20
        ),
    )(features, tile_row, tile_col, tile_count, tile_vals, weight, cotangent)


def solution(mesh):
    return jax.shard_map(
        on_device,
        mesh=mesh,
        in_specs=(
            P(("col", "row"), None),
            P("row", "col", None),
            P("row", "col", None),
            P("row", "col"),
            P("row", "col", None, None, None),
            P(),
            P(("row", "col"), None),
        ),
        out_specs=(P(("row", "col"), None), P()),
        check_vma=False,
    )
```

```python
import jax
import jax.numpy as jnp
from jax import lax
from jax.experimental import pallas as pl
from jax.experimental.pallas import tpu as pltpu
from jax.sharding import PartitionSpec as P

NY, NXL, NXH, NZ, NC = 8, 2, 4, 8, 2
NX = NXH * NXL
S = 128
SLOTS = 96
ROWS = 64
UNROLL = 32
COLS = 16
FAR_FIRST = (4, 3, 5, 2, 6, 1, 7)
NEAR_FIRST = (1, 7, 2, 6, 3, 5, 4)
X_OFF = (2, 1, 3, 0)
PIECES = ((0, 24), (24, 24), (48, 16))
BF, F32, I32 = jnp.bfloat16, jnp.float32, jnp.int32


def span_right(k):
    return 4 if k % 2 == 0 else 3


def span_left(k):
    return 3 if k % 2 == 0 else 4


def wrap(value, size):
    return lax.rem(value + size, size)


def kernel(
    count_ref, feat_hbm, row_hbm, col_hbm, vals_hbm, weight_hbm, cot_hbm,
    out_ref, grad_ref,
    feat_ref, row_ref, col_ref, weight_ref, cot_ref, vals, gath, prefix, meta_v, meta_s, core_out, core_in, pair, z_out, z_in,
    x_out, x_in, part, half, half_in, stage_out, stage_in, full_in,
    in_sem, meta_sem, g_send, g_recv, c_send, c_recv, z_send, z_recv,
    x_send, x_recv, w_send, w_recv, e_send, e_recv,
):
    row, col = lax.axis_index("row"), lax.axis_index("col")
    y, xl = lax.div(row, NXL), lax.rem(row, NXL)
    xh, z, c = lax.div(col, NZ * NC), lax.rem(lax.div(col, NC), NZ), lax.rem(col, NC)
    x = xh * NXL + xl

    def device(y=y, x=x, z=z, c=c):
        return {
            "row": y * NXL + lax.rem(x, NXL),
            "col": lax.div(x, NXL) * (NZ * NC) + z * NC + c,
        }

    def send(src, dst, send_sem, recv_sem, to):
        copy = pltpu.make_async_remote_copy(
            src_ref=src, dst_ref=dst, send_sem=send_sem, recv_sem=recv_sem,
            device_id=to, device_id_type=pl.DeviceIdType.MESH,
        )
        copy.start()
        return copy

    barrier = pltpu.get_barrier_semaphore()
    peers = [device(c=1 - c)]
    for k in FAR_FIRST:
        peers += [device(y=wrap(y + k, NY)), device(x=wrap(x + k, NX)), device(z=wrap(z + k, NZ))]
    for peer in peers:
        pl.semaphore_signal(barrier, inc=1, device_id=peer, device_id_type=pl.DeviceIdType.MESH)

    loads = [
        pltpu.make_async_copy(src, dst, in_sem.at[i])
        for i, (src, dst) in enumerate((
            (feat_hbm, feat_ref), (row_hbm, row_ref), (col_hbm, col_ref),
            (vals_hbm.at[0, 0], vals), (weight_hbm, weight_ref), (cot_hbm, cot_ref),
        ))
    ]
    for copy in loads:
        copy.start()
    for copy in loads[:3]:
        copy.wait()

    lane = lax.broadcasted_iota(I32, (SLOTS, SLOTS), 1)
    sub = lax.broadcasted_iota(I32, (SLOTS, SLOTS), 0)
    lane1 = lax.broadcasted_iota(I32, (1, SLOTS), 1)
    live = lane1 < count_ref[0, 0]
    trow = jnp.where(live, row_ref[0], ROWS)
    tcol = jnp.where(live, col_ref[0], 0)
    trow_b = jnp.broadcast_to(trow, (SLOTS, SLOTS))
    diagonal = lane == sub
    trow_c = jnp.sum(jnp.where(diagonal, trow_b, 0), axis=1, keepdims=True)
    tcol_c = jnp.sum(jnp.where(diagonal, jnp.broadcast_to(tcol, (SLOTS, SLOTS)), 0), axis=1, keepdims=True)
    before = (trow_b < trow_c) | ((trow_b == trow_c) & (lane < sub))
    rank_c = jnp.sum(jnp.where(before, 1, 0), axis=1, keepdims=True)
    same_c = jnp.max(jnp.where((trow_b == trow_c) & (lane < sub), 1, 0), axis=1, keepdims=True)
    place = rank_c == lane
    slot_s = jnp.sum(jnp.where(place, sub, 0), axis=0, keepdims=True)
    col_s = jnp.sum(jnp.where(place, jnp.broadcast_to(tcol_c, (SLOTS, SLOTS)), 0), axis=0, keepdims=True)
    same_s = jnp.sum(jnp.where(place, jnp.broadcast_to(same_c, (SLOTS, SLOTS)), 0), axis=0, keepdims=True)
    upto = jnp.sum(jnp.where(trow_c <= lane, 1, 0), axis=0, keepdims=True)
    held = jnp.sum(jnp.where(trow_c == lane, 1, 0), axis=0, keepdims=True)
    end_s = jnp.where(held > 0, upto - 1, SLOTS)
    meta_v[...] = jnp.zeros_like(meta_v)
    meta_v[0:1, :SLOTS] = slot_s
    meta_v[1:2, :SLOTS] = col_s
    meta_v[2:3, :SLOTS] = same_s
    meta_v[3:4, :SLOTS] = end_s
    to_scalars = pltpu.make_async_copy(meta_v, meta_s, meta_sem)
    to_scalars.start()

    gath[row] = feat_ref[...]
    prefix[SLOTS] = jnp.zeros((S, S), F32)

    pl.semaphore_wait(barrier, len(peers))

    sent = []
    partner = device(x=xh * NXL + 1 - xl)
    along = {}
    across = [send(feat_ref, gath.at[row], g_send.at[8], g_recv.at[8], partner)]
    for k in FAR_FIRST:
        along[k] = send(feat_ref, gath.at[row], g_send.at[k], g_recv.at[k], device(y=wrap(y + k, NY)))
    for k in NEAR_FIRST:
        along[k].wait_recv()
        block = wrap(y - k, NY) * NXL + xl
        across.append(send(gath.at[block], gath.at[block], g_send.at[8 + k], g_recv.at[8 + k], partner))
    to_scalars.wait()
    for copy in loads[3:]:
        copy.wait()
    for copy in across:
        copy.wait_recv()
    sent += list(along.values()) + across

    def group(g, running):
        first = g * UNROLL
        for u in range(UNROLL):
            s = first + u
            product = jnp.dot(vals[meta_s[0, s]], gath[meta_s[1, s]], preferred_element_type=F32)
            running = running * meta_s[2, s].astype(F32) + product
            prefix[s] = running
        return running

    lax.fori_loop(0, SLOTS // UNROLL, group, jnp.zeros((S, S), F32))

    def tile_row(dz, k, core):
        return wrap(xh + X_OFF[k], NXH) * (NZ * NC) + wrap(z + dz, NZ) * NC + core

    swaps = {}
    other = device(c=1 - c)
    for dz in FAR_FIRST + (0,):
        for k in range(NXH):
            core_out[dz, k] = prefix[meta_s[3, tile_row(dz, k, 1 - c)]].astype(BF)
        swaps[dz] = send(core_out.at[dz], core_in.at[dz], c_send.at[dz], c_recv.at[dz], other)
    ready = set()

    def pair_sum(dz):
        if dz not in ready:
            ready.add(dz)
            swaps[dz].wait_recv()
            for k in range(NXH):
                pair[dz, k] = core_in[dz, k].astype(F32) + prefix[meta_s[3, tile_row(dz, k, c)]]

    right, left = device(z=wrap(z + 1, NZ)), device(z=wrap(z - 1, NZ))
    rings = {}
    for step in range(1, 5):
        for k in range(NXH):
            for way, span, sign, to in ((0, span_right(k), 1, right), (1, span_left(k), -1, left)):
                at = step - (4 - span)
                if at < 1:
                    continue
                dz = (sign * (span - at + 1)) % NZ
                pair_sum(dz)
                total = pair[dz, k]
                if at > 1:
                    rings[way, k, step - 1].wait_recv()
                    total = total + z_in[way, k, step - 2].astype(F32)
                z_out[way, k, step - 1] = total.astype(BF)
                rings[way, k, step] = send(
                    z_out.at[way, k, step - 1], z_in.at[way, k, step - 1],
                    z_send.at[way, k, step - 1], z_recv.at[way, k, step - 1], to,
                )
    sent += list(swaps.values())

    pair_sum(0)
    hops = []
    for k in range(NXH):
        rings[0, k, 4].wait_recv()
        rings[1, k, 4].wait_recv()
        total = pair[0, k] + z_in[0, k, 3].astype(F32) + z_in[1, k, 3].astype(F32)
        if X_OFF[k]:
            x_out[k] = total.astype(BF)
            to = device(x=wrap(xh + X_OFF[k], NXH) * NXL + xl)
            hops.append(send(x_out.at[k], x_in.at[k], x_send.at[k], x_recv.at[k], to))
    for k, copy in enumerate(hops):
        copy.wait_recv()
        total = total + x_in[k].astype(F32)
    sent += list(rings.values()) + hops

    aggregated = total.astype(BF)
    pre = jnp.dot(aggregated, weight_ref[...], preferred_element_type=F32)
    sigmoid_pre = jax.nn.sigmoid(pre)
    out_ref[...] = (pre * sigmoid_pre).astype(BF)
    derivative = sigmoid_pre * (1.0 + pre * (1.0 - sigmoid_pre))
    grad_pre = (cot_ref[...].astype(F32) * derivative).astype(BF)
    part[...] = lax.dot_general(aggregated, grad_pre, (((0,), (0,)), ((), ())), preferred_element_type=F32)

    mine = pl.ds(pl.multiple_of(c * (S // 2), S // 2), S // 2)
    theirs = pl.ds(pl.multiple_of((1 - c) * (S // 2), S // 2), S // 2)
    swap = send(part.at[theirs], half_in, e_send.at[0], e_recv.at[0], other)
    swap.wait_recv()
    half[...] = part[mine] + half_in[...]
    sent.append(swap)
    axes = (
        (z, lambda k: device(z=wrap(z + k, NZ))),
        (x, lambda k: device(x=wrap(x + k, NX))),
        (y, lambda k: device(y=wrap(y + k, NY))),
    )
    for stage in range(3):
        copies = []
        for p, (start, size) in enumerate(PIECES):
            stage_out[stage, pl.ds(start, size)] = half[pl.ds(start, size)]
        for k in FAR_FIRST:
            for p, (start, size) in enumerate(PIECES):
                place_on, to = axes[(stage + p) % 3]
                rows = pl.ds(start, size)
                copies.append(send(
                    stage_out.at[stage, rows], stage_in.at[stage, place_on, rows],
                    w_send.at[stage, p, k], w_recv.at[stage, p, k], to(k),
                ))
        for p, (start, size) in enumerate(PIECES):
            rows = pl.ds(start, size)
            stage_in[stage, axes[(stage + p) % 3][0], rows] = half[rows]
        for copy in sent:
            copy.wait_send()
        for copy in copies:
            copy.wait_recv()
        total = stage_in[stage, 0]
        for n in range(1, 8):
            total = total + stage_in[stage, n]
        half[...] = total
        sent = copies
    swap = send(half, full_in, e_send.at[1], e_recv.at[1], other)
    grad_ref[mine] = half[...]
    for copy in sent:
        copy.wait_send()
    swap.wait()
    grad_ref[theirs] = full_in[...]


def on_device(features, tile_row, tile_col, tile_count, tile_vals, weight, cotangent):
    vmem = pl.BlockSpec(memory_space=pltpu.VMEM)
    dma = pltpu.SemaphoreType.DMA
    return pl.pallas_call(
        kernel,
        out_shape=(jax.ShapeDtypeStruct((S, S), BF), jax.ShapeDtypeStruct((S, S), F32)),
        in_specs=[pl.BlockSpec(memory_space=pltpu.SMEM)] + [pl.BlockSpec(memory_space=pltpu.HBM)] * 6,
        out_specs=(vmem, vmem),
        scratch_shapes=[
            pltpu.VMEM((S, S), BF),
            pltpu.VMEM((1, 1, SLOTS), I32),
            pltpu.VMEM((1, 1, SLOTS), I32),
            pltpu.VMEM((S, S), BF),
            pltpu.VMEM((S, S), BF),
            pltpu.VMEM((SLOTS, S, S), BF),
            pltpu.VMEM((COLS, S, S), BF),
            pltpu.VMEM((SLOTS + 1, S, S), F32),
            pltpu.VMEM((8, S), I32),
            pltpu.SMEM((8, S), I32),
            pltpu.VMEM((NZ, NXH, S, S), BF),
            pltpu.VMEM((NZ, NXH, S, S), BF),
            pltpu.VMEM((NZ, NXH, S, S), F32),
            pltpu.VMEM((2, NXH, 4, S, S), BF),
            pltpu.VMEM((2, NXH, 4, S, S), BF),
            pltpu.VMEM((3, S, S), BF),
            pltpu.VMEM((3, S, S), BF),
            pltpu.VMEM((S, S), F32),
            pltpu.VMEM((S // 2, S), F32),
            pltpu.VMEM((S // 2, S), F32),
            pltpu.VMEM((3, S // 2, S), F32),
            pltpu.VMEM((3, 8, S // 2, S), F32),
            pltpu.VMEM((S // 2, S), F32),
            dma((6,)), dma,
            dma((16,)), dma((16,)),
            dma((NZ,)), dma((NZ,)),
            dma((2, NXH, 4)), dma((2, NXH, 4)),
            dma((3,)), dma((3,)),
            dma((3, 3, 8)), dma((3, 3, 8)),
            dma((2,)), dma((2,)),
        ],
        compiler_params=pltpu.CompilerParams(
            collective_id=0, has_side_effects=True, vmem_limit_bytes=40 * 2**20
        ),
    )(tile_count, *(
        pltpu.with_memory_space_constraint(value, pltpu.HBM)
        for value in (features, tile_row, tile_col, tile_vals, weight, cotangent)
    ))


def solution(mesh):
    return jax.shard_map(
        on_device,
        mesh=mesh,
        in_specs=(
            P(("col", "row"), None),
            P("row", "col", None),
            P("row", "col", None),
            P("row", "col"),
            P("row", "col", None, None, None),
            P(),
            P(("row", "col"), None),
        ),
        out_specs=(P(("row", "col"), None), P()),
        check_vma=False,
    )
```

```python
import jax
import jax.numpy as jnp
from jax import lax
from jax.experimental import pallas as pl
from jax.experimental.pallas import tpu as pltpu
from jax.sharding import PartitionSpec as P

NY, NXL, NXH, NZ, NC = 8, 2, 4, 8, 2
NX = NXH * NXL
S = 128
SLOTS = 96
ROWS = 64
UNROLL = 32
COLS = 16
FAR_FIRST = (4, 3, 5, 2, 6, 1, 7)
X_OFF = (2, 1, 3, 0)
PIECES = ((0, 24), (24, 24), (48, 16))
BF, F32, I32 = jnp.bfloat16, jnp.float32, jnp.int32


def span_right(k):
    return 4 if k % 2 == 0 else 3


def span_left(k):
    return 3 if k % 2 == 0 else 4


def wrap(value, size):
    return lax.rem(value + size, size)


def kernel(
    count_ref, feat_hbm, row_hbm, col_hbm, vals_hbm, weight_hbm, cot_hbm,
    out_ref, grad_ref,
    feat_ref, row_ref, col_ref, weight_ref, cot_ref, vals, gath, prefix, meta_v, meta_s, core_out, core_in, pair, z_out, z_in,
    x_out, x_in, part, half, half_in, stage_out, stage_in, full_in,
    in_sem, meta_sem, g_send, g_recv, c_send, c_recv, z_send, z_recv,
    x_send, x_recv, x_near, w_send, w_recv, e_send, e_recv,
):
    row, col = lax.axis_index("row"), lax.axis_index("col")
    y, xl = lax.div(row, NXL), lax.rem(row, NXL)
    xh, z, c = lax.div(col, NZ * NC), lax.rem(lax.div(col, NC), NZ), lax.rem(col, NC)
    x = xh * NXL + xl

    def device(y=y, x=x, z=z, c=c):
        return {
            "row": y * NXL + lax.rem(x, NXL),
            "col": lax.div(x, NXL) * (NZ * NC) + z * NC + c,
        }

    def send(src, dst, send_sem, recv_sem, to):
        copy = pltpu.make_async_remote_copy(
            src_ref=src, dst_ref=dst, send_sem=send_sem, recv_sem=recv_sem,
            device_id=to, device_id_type=pl.DeviceIdType.MESH,
        )
        copy.start()
        return copy

    barrier = pltpu.get_barrier_semaphore()
    partner = device(x=xh * NXL + 1 - xl)
    peers = [partner, device(c=1 - c)]
    for k in (1, -1):
        peers += [device(z=wrap(z + k, NZ)), device(x=wrap(x + k * NXL, NX))]
    for k in (1, -1, 2, -2):
        peers += [device(y=wrap(y + k, NY)), device(y=wrap(y + k, NY), x=xh * NXL + 1 - xl)]
    for peer in peers:
        pl.semaphore_signal(barrier, inc=1, device_id=peer, device_id_type=pl.DeviceIdType.MESH)

    loads = [
        pltpu.make_async_copy(src, dst, in_sem.at[i])
        for i, (src, dst) in enumerate((
            (feat_hbm, feat_ref), (row_hbm, row_ref), (col_hbm, col_ref),
            (vals_hbm.at[0, 0], vals), (weight_hbm, weight_ref), (cot_hbm, cot_ref),
        ))
    ]
    for copy in loads:
        copy.start()
    for copy in loads[:3]:
        copy.wait()

    lane = lax.broadcasted_iota(I32, (SLOTS, SLOTS), 1)
    sub = lax.broadcasted_iota(I32, (SLOTS, SLOTS), 0)
    lane1 = lax.broadcasted_iota(I32, (1, SLOTS), 1)
    live = lane1 < count_ref[0, 0]
    trow = jnp.where(live, row_ref[0], ROWS)
    tcol = jnp.where(live, col_ref[0], 0)
    trow_b = jnp.broadcast_to(trow, (SLOTS, SLOTS))
    diagonal = lane == sub
    trow_c = jnp.sum(jnp.where(diagonal, trow_b, 0), axis=1, keepdims=True)
    tcol_c = jnp.sum(jnp.where(diagonal, jnp.broadcast_to(tcol, (SLOTS, SLOTS)), 0), axis=1, keepdims=True)
    before = (trow_b < trow_c) | ((trow_b == trow_c) & (lane < sub))
    rank_c = jnp.sum(jnp.where(before, 1, 0), axis=1, keepdims=True)
    same_c = jnp.max(jnp.where((trow_b == trow_c) & (lane < sub), 1, 0), axis=1, keepdims=True)
    place = rank_c == lane
    slot_s = jnp.sum(jnp.where(place, sub, 0), axis=0, keepdims=True)
    col_s = jnp.sum(jnp.where(place, jnp.broadcast_to(tcol_c, (SLOTS, SLOTS)), 0), axis=0, keepdims=True)
    same_s = jnp.sum(jnp.where(place, jnp.broadcast_to(same_c, (SLOTS, SLOTS)), 0), axis=0, keepdims=True)
    upto = jnp.sum(jnp.where(trow_c <= lane, 1, 0), axis=0, keepdims=True)
    held = jnp.sum(jnp.where(trow_c == lane, 1, 0), axis=0, keepdims=True)
    end_s = jnp.where(held > 0, upto - 1, SLOTS)
    meta_v[...] = jnp.zeros_like(meta_v)
    meta_v[0:1, :SLOTS] = slot_s
    meta_v[1:2, :SLOTS] = col_s
    meta_v[2:3, :SLOTS] = same_s
    meta_v[3:4, :SLOTS] = end_s
    to_scalars = pltpu.make_async_copy(meta_v, meta_s, meta_sem)
    to_scalars.start()

    gath[row] = feat_ref[...]
    prefix[SLOTS] = jnp.zeros((S, S), F32)

    pl.semaphore_wait(barrier, len(peers))

    pl.semaphore_signal(
        x_near, inc=1, device_id=device(x=wrap(x + NXL, NX)), device_id_type=pl.DeviceIdType.MESH
    )

    def block_from(k):
        return wrap(y - k, NY) * NXL + xl

    along, across = {}, []

    def hand_on(k, to, index, rows=pl.ds(0, S)):
        part = gath.at[block_from(k), rows]
        return send(part, part, g_send.at[index], g_recv.at[index], to)

    across.append(send(feat_ref, gath.at[row], g_send.at[8], g_recv.at[8], partner))
    for k in (2, 6, 1, 7):
        along[k] = send(feat_ref, gath.at[row], g_send.at[k], g_recv.at[k], device(y=wrap(y + k, NY)))
    for k, step, rows, half_at, half_across, whole_at in (
        (2, 1, pl.ds(0, S // 2), 4, 12, 3),
        (6, -1, pl.ds(S // 2, S // 2), 0, 16, 5),
    ):
        two, one = wrap(y + 2 * step, NY), wrap(y + step, NY)
        other_x = xh * NXL + 1 - xl
        along[k].wait_recv()
        along[half_at] = hand_on(k, device(y=two), half_at, rows)
        across.append(hand_on(k, device(y=two, x=other_x), half_across, rows))
        along[whole_at] = hand_on(k, device(y=one), whole_at)
        across.append(hand_on(k, device(y=one, x=other_x), 8 + whole_at))
        across.append(hand_on(k, partner, 8 + k))
    for k in (1, 7):
        along[k].wait_recv()
        across.append(hand_on(k, partner, 8 + k))
    for k in (3, 5, 4, 0):
        along[k].wait_recv()
    to_scalars.wait()
    for copy in loads[3:]:
        copy.wait()
    for copy in across:
        copy.wait_recv()
    sent = list(along.values()) + across

    def group(g, running):
        first = g * UNROLL
        for u in range(UNROLL):
            s = first + u
            product = jnp.dot(vals[meta_s[0, s]], gath[meta_s[1, s]], preferred_element_type=F32)
            running = running * meta_s[2, s].astype(F32) + product
            prefix[s] = running
        return running

    lax.fori_loop(0, SLOTS // UNROLL, group, jnp.zeros((S, S), F32))

    def tile_row(dz, k, core):
        return wrap(xh + X_OFF[k], NXH) * (NZ * NC) + wrap(z + dz, NZ) * NC + core

    swaps = {}
    other = device(c=1 - c)
    for dz in FAR_FIRST + (0,):
        for k in range(NXH):
            core_out[dz, k] = prefix[meta_s[3, tile_row(dz, k, 1 - c)]].astype(BF)
        swaps[dz] = send(core_out.at[dz], core_in.at[dz], c_send.at[dz], c_recv.at[dz], other)
    ready = set()

    def pair_sum(dz):
        if dz not in ready:
            ready.add(dz)
            swaps[dz].wait_recv()
            for k in range(NXH):
                pair[dz, k] = core_in[dz, k].astype(F32) + prefix[meta_s[3, tile_row(dz, k, c)]]

    right, left = device(z=wrap(z + 1, NZ)), device(z=wrap(z - 1, NZ))
    rings = {}
    for step in range(1, 5):
        for k in range(NXH):
            for way, span, sign, to in ((0, span_right(k), 1, right), (1, span_left(k), -1, left)):
                at = step - (4 - span)
                if at < 1:
                    continue
                dz = (sign * (span - at + 1)) % NZ
                pair_sum(dz)
                total = pair[dz, k]
                if at > 1:
                    rings[way, k, step - 1].wait_recv()
                    total = total + z_in[way, k, step - 2].astype(F32)
                z_out[way, k, step - 1] = total.astype(BF)
                rings[way, k, step] = send(
                    z_out.at[way, k, step - 1], z_in.at[way, k, step - 1],
                    z_send.at[way, k, step - 1], z_recv.at[way, k, step - 1], to,
                )
    sent += list(swaps.values())

    pl.semaphore_wait(x_near, 1)
    pair_sum(0)
    hops = []
    for k in range(NXH):
        rings[0, k, 4].wait_recv()
        rings[1, k, 4].wait_recv()
        total = pair[0, k] + z_in[0, k, 3].astype(F32) + z_in[1, k, 3].astype(F32)
        if X_OFF[k]:
            x_out[k] = total.astype(BF)
            to = device(x=wrap(xh + X_OFF[k], NXH) * NXL + xl)
            hops.append(send(x_out.at[k], x_in.at[k], x_send.at[k], x_recv.at[k], to))
    for k, copy in enumerate(hops):
        copy.wait_recv()
        total = total + x_in[k].astype(F32)
    sent += list(rings.values()) + hops

    aggregated = total.astype(BF)
    pre = jnp.dot(aggregated, weight_ref[...], preferred_element_type=F32)
    sigmoid_pre = jax.nn.sigmoid(pre)
    out_ref[...] = (pre * sigmoid_pre).astype(BF)
    derivative = sigmoid_pre * (1.0 + pre * (1.0 - sigmoid_pre))
    grad_pre = (cot_ref[...].astype(F32) * derivative).astype(BF)
    part[...] = lax.dot_general(aggregated, grad_pre, (((0,), (0,)), ((), ())), preferred_element_type=F32)

    mine = pl.ds(pl.multiple_of(c * (S // 2), S // 2), S // 2)
    theirs = pl.ds(pl.multiple_of((1 - c) * (S // 2), S // 2), S // 2)
    swap = send(part.at[theirs], half_in, e_send.at[0], e_recv.at[0], other)
    swap.wait_recv()
    half[...] = part[mine] + half_in[...]
    sent.append(swap)
    axes = (
        (z, lambda k: device(z=wrap(z + k, NZ))),
        (x, lambda k: device(x=wrap(x + k, NX))),
        (y, lambda k: device(y=wrap(y + k, NY))),
    )
    for stage in range(3):
        copies = []
        for p, (start, size) in enumerate(PIECES):
            stage_out[stage, pl.ds(start, size)] = half[pl.ds(start, size)]
        for k in FAR_FIRST:
            for p, (start, size) in enumerate(PIECES):
                place_on, to = axes[(stage + p) % 3]
                rows = pl.ds(start, size)
                copies.append(send(
                    stage_out.at[stage, rows], stage_in.at[stage, place_on, rows],
                    w_send.at[stage, p, k], w_recv.at[stage, p, k], to(k),
                ))
        for p, (start, size) in enumerate(PIECES):
            rows = pl.ds(start, size)
            stage_in[stage, axes[(stage + p) % 3][0], rows] = half[rows]
        for copy in sent:
            copy.wait_send()
        for copy in copies:
            copy.wait_recv()
        total = stage_in[stage, 0]
        for n in range(1, 8):
            total = total + stage_in[stage, n]
        half[...] = total
        sent = copies
    swap = send(half, full_in, e_send.at[1], e_recv.at[1], other)
    grad_ref[mine] = half[...]
    for copy in sent:
        copy.wait_send()
    swap.wait()
    grad_ref[theirs] = full_in[...]


def on_device(features, tile_row, tile_col, tile_count, tile_vals, weight, cotangent):
    vmem = pl.BlockSpec(memory_space=pltpu.VMEM)
    dma = pltpu.SemaphoreType.DMA
    return pl.pallas_call(
        kernel,
        out_shape=(jax.ShapeDtypeStruct((S, S), BF), jax.ShapeDtypeStruct((S, S), F32)),
        in_specs=[pl.BlockSpec(memory_space=pltpu.SMEM)] + [pl.BlockSpec(memory_space=pltpu.HBM)] * 6,
        out_specs=(vmem, vmem),
        scratch_shapes=[
            pltpu.VMEM((S, S), BF),
            pltpu.VMEM((1, 1, SLOTS), I32),
            pltpu.VMEM((1, 1, SLOTS), I32),
            pltpu.VMEM((S, S), BF),
            pltpu.VMEM((S, S), BF),
            pltpu.VMEM((SLOTS, S, S), BF),
            pltpu.VMEM((COLS, S, S), BF),
            pltpu.VMEM((SLOTS + 1, S, S), F32),
            pltpu.VMEM((8, S), I32),
            pltpu.SMEM((8, S), I32),
            pltpu.VMEM((NZ, NXH, S, S), BF),
            pltpu.VMEM((NZ, NXH, S, S), BF),
            pltpu.VMEM((NZ, NXH, S, S), F32),
            pltpu.VMEM((2, NXH, 4, S, S), BF),
            pltpu.VMEM((2, NXH, 4, S, S), BF),
            pltpu.VMEM((3, S, S), BF),
            pltpu.VMEM((3, S, S), BF),
            pltpu.VMEM((S, S), F32),
            pltpu.VMEM((S // 2, S), F32),
            pltpu.VMEM((S // 2, S), F32),
            pltpu.VMEM((3, S // 2, S), F32),
            pltpu.VMEM((3, 8, S // 2, S), F32),
            pltpu.VMEM((S // 2, S), F32),
            dma((6,)), dma,
            dma((17,)), dma((17,)),
            dma((NZ,)), dma((NZ,)),
            dma((2, NXH, 4)), dma((2, NXH, 4)),
            dma((3,)), dma((3,)), pltpu.SemaphoreType.REGULAR,
            dma((3, 3, 8)), dma((3, 3, 8)),
            dma((2,)), dma((2,)),
        ],
        compiler_params=pltpu.CompilerParams(
            collective_id=0, has_side_effects=True, vmem_limit_bytes=40 * 2**20
        ),
    )(tile_count, *(
        pltpu.with_memory_space_constraint(value, pltpu.HBM)
        for value in (features, tile_row, tile_col, tile_vals, weight, cotangent)
    ))


def solution(mesh):
    return jax.shard_map(
        on_device,
        mesh=mesh,
        in_specs=(
            P(("col", "row"), None),
            P("row", "col", None),
            P("row", "col", None),
            P("row", "col"),
            P("row", "col", None, None, None),
            P(),
            P(("row", "col"), None),
        ),
        out_specs=(P(("row", "col"), None), P()),
        check_vma=False,
    )
```

```python
import jax
import jax.numpy as jnp
from jax import lax
from jax.experimental import pallas as pl
from jax.experimental.pallas import tpu as pltpu
from jax.sharding import PartitionSpec as P

NY, NXL, NXH, NZ, NC = 8, 2, 4, 8, 2
NX = NXH * NXL
S = 128
SLOTS = 96
ROWS = 64
UNROLL = 48
COLS = 16
FAR_FIRST = (4, 3, 5, 2, 6, 1, 7)
X_OFF = (2, 1, 3, 0)
PIECES = ((0, 24), (24, 24), (48, 16))
BF, F32, I32 = jnp.bfloat16, jnp.float32, jnp.int32


def ring_plan(sign):
    long = {0: (4, 1, ()), 1: (3, 1, (0,)), 2: (2, 1, (1,)), 3: (1, 1, (2,))}
    short = {4: (-3, -1, ()), 5: (-2, -1, (4,)), 6: (-1, -1, (5,))}
    return {slot: (sign * ahead, sign * hop, needs) for slot, (ahead, hop, needs) in {**long, **short}.items()}


RINGS = (ring_plan(1), ring_plan(1), ring_plan(-1), ring_plan(-1))
LAST = (3, 6)
RING_ORDER = (
    ((0, 0), (0, 4), (1, 0), (1, 4), (2, 0), (2, 4), (3, 0), (3, 4)),
    ((0, 1), (0, 5), (1, 1), (1, 5), (2, 1), (2, 5), (3, 1), (3, 5)),
    ((0, 2), (0, 6), (1, 2), (1, 6), (2, 2), (2, 6), (3, 2), (3, 6)),
    ((0, 3), (1, 3), (2, 3), (3, 3)),
)


def wrap(value, size):
    return lax.rem(value + size, size)


def kernel(
    count_ref, feat_hbm, row_hbm, col_hbm, vals_hbm, weight_hbm, cot_hbm,
    out_ref, grad_ref,
    feat_ref, row_ref, col_ref, weight_ref, cot_ref, vals, gath, prefix, meta_v, meta_s, core_out, core_in, pair, z_out, z_in,
    x_out, x_in, part, half, half_in, stage_out, stage_in, full_in,
    in_sem, meta_sem, g_send, g_recv, c_send, c_recv, z_send, z_recv,
    x_send, x_recv, x_near, w_send, w_recv, e_send, e_recv,
):
    row, col = lax.axis_index("row"), lax.axis_index("col")
    y, xl = lax.div(row, NXL), lax.rem(row, NXL)
    xh, z, c = lax.div(col, NZ * NC), lax.rem(lax.div(col, NC), NZ), lax.rem(col, NC)
    x = xh * NXL + xl

    def device(y=y, x=x, z=z, c=c):
        return {
            "row": y * NXL + lax.rem(x, NXL),
            "col": lax.div(x, NXL) * (NZ * NC) + z * NC + c,
        }

    def send(src, dst, send_sem, recv_sem, to):
        copy = pltpu.make_async_remote_copy(
            src_ref=src, dst_ref=dst, send_sem=send_sem, recv_sem=recv_sem,
            device_id=to, device_id_type=pl.DeviceIdType.MESH,
        )
        copy.start()
        return copy

    barrier = pltpu.get_barrier_semaphore()
    partner = device(x=xh * NXL + 1 - xl)
    peers = [partner, device(c=1 - c)]
    for k in (1, -1):
        peers += [device(z=wrap(z + k, NZ)), device(x=wrap(x + k * NXL, NX))]
    for k in (1, -1, 2, -2):
        peers += [device(y=wrap(y + k, NY)), device(y=wrap(y + k, NY), x=xh * NXL + 1 - xl)]
    for peer in peers:
        pl.semaphore_signal(barrier, inc=1, device_id=peer, device_id_type=pl.DeviceIdType.MESH)

    loads = [
        pltpu.make_async_copy(src, dst, in_sem.at[i])
        for i, (src, dst) in enumerate((
            (feat_hbm, feat_ref), (row_hbm, row_ref), (col_hbm, col_ref),
            (vals_hbm.at[0, 0], vals), (weight_hbm, weight_ref), (cot_hbm, cot_ref),
        ))
    ]
    for copy in loads:
        copy.start()
    pl.semaphore_wait(barrier, len(peers))

    pl.semaphore_signal(
        x_near, inc=1, device_id=device(x=wrap(x + NXL, NX)), device_id_type=pl.DeviceIdType.MESH
    )

    def block_from(k):
        return wrap(y - k, NY) * NXL + xl

    along, across = {}, []

    def hand_on(k, to, index, rows=pl.ds(0, S)):
        part = gath.at[block_from(k), rows]
        return send(part, part, g_send.at[index], g_recv.at[index], to)

    across.append(send(feat_hbm, gath.at[row], g_send.at[8], g_recv.at[8], partner))
    for k in (2, 6, 1, 7):
        along[k] = send(feat_hbm, gath.at[row], g_send.at[k], g_recv.at[k], device(y=wrap(y + k, NY)))

    for copy in loads[:3]:
        copy.wait()

    lane = lax.broadcasted_iota(I32, (SLOTS, SLOTS), 1)
    sub = lax.broadcasted_iota(I32, (SLOTS, SLOTS), 0)
    lane1 = lax.broadcasted_iota(I32, (1, SLOTS), 1)
    live = lane1 < count_ref[0, 0]
    trow = jnp.where(live, row_ref[0], ROWS)
    tcol = jnp.where(live, col_ref[0], 0)
    trow_b = jnp.broadcast_to(trow, (SLOTS, SLOTS))
    diagonal = lane == sub
    trow_c = jnp.sum(jnp.where(diagonal, trow_b, 0), axis=1, keepdims=True)
    tcol_c = jnp.sum(jnp.where(diagonal, jnp.broadcast_to(tcol, (SLOTS, SLOTS)), 0), axis=1, keepdims=True)
    before = (trow_b < trow_c) | ((trow_b == trow_c) & (lane < sub))
    rank_c = jnp.sum(jnp.where(before, 1, 0), axis=1, keepdims=True)
    same_c = jnp.max(jnp.where((trow_b == trow_c) & (lane < sub), 1, 0), axis=1, keepdims=True)
    place = rank_c == lane
    slot_s = jnp.sum(jnp.where(place, sub, 0), axis=0, keepdims=True)
    col_s = jnp.sum(jnp.where(place, jnp.broadcast_to(tcol_c, (SLOTS, SLOTS)), 0), axis=0, keepdims=True)
    same_s = jnp.sum(jnp.where(place, jnp.broadcast_to(same_c, (SLOTS, SLOTS)), 0), axis=0, keepdims=True)
    upto = jnp.sum(jnp.where(trow_c <= lane, 1, 0), axis=0, keepdims=True)
    held = jnp.sum(jnp.where(trow_c == lane, 1, 0), axis=0, keepdims=True)
    end_s = jnp.where(held > 0, upto - 1, SLOTS)
    meta_v[...] = jnp.zeros_like(meta_v)
    meta_v[0:1, :SLOTS] = slot_s
    meta_v[1:2, :SLOTS] = col_s
    meta_v[2:3, :SLOTS] = same_s
    meta_v[3:4, :SLOTS] = end_s
    to_scalars = pltpu.make_async_copy(meta_v, meta_s, meta_sem)
    to_scalars.start()
    gath[row] = feat_ref[...]

    prefix[SLOTS] = jnp.zeros((S, S), F32)

    for k, step, rows, half_at, half_across, whole_at in (
        (2, 1, pl.ds(0, S // 2), 4, 12, 3),
        (6, -1, pl.ds(S // 2, S // 2), 0, 16, 5),
    ):
        two, one = wrap(y + 2 * step, NY), wrap(y + step, NY)
        other_x = xh * NXL + 1 - xl
        along[k].wait_recv()
        along[half_at] = hand_on(k, device(y=two), half_at, rows)
        across.append(hand_on(k, device(y=two, x=other_x), half_across, rows))
        along[whole_at] = hand_on(k, device(y=one), whole_at)
        across.append(hand_on(k, device(y=one, x=other_x), 8 + whole_at))
        across.append(hand_on(k, partner, 8 + k))
    for k in (1, 7):
        along[k].wait_recv()
        across.append(hand_on(k, partner, 8 + k))
    for k in (3, 5, 4, 0):
        along[k].wait_recv()
    to_scalars.wait()
    for copy in loads[3:]:
        copy.wait()
    for copy in across:
        copy.wait_recv()
    sent = list(along.values()) + across

    def group(g, running):
        first = g * UNROLL
        for u in range(UNROLL):
            s = first + u
            product = jnp.dot(vals[meta_s[0, s]], gath[meta_s[1, s]], preferred_element_type=F32)
            running = running * meta_s[2, s].astype(F32) + product
            prefix[s] = running
        return running

    lax.fori_loop(0, SLOTS // UNROLL, group, jnp.zeros((S, S), F32))

    def tile_row(dz, k, core):
        return wrap(xh + X_OFF[k], NXH) * (NZ * NC) + wrap(z + dz, NZ) * NC + core

    swaps = {}
    other = device(c=1 - c)
    for dz in FAR_FIRST + (0,):
        for k in range(NXH):
            core_out[dz, k] = prefix[meta_s[3, tile_row(dz, k, 1 - c)]].astype(BF)
        swaps[dz] = send(core_out.at[dz], core_in.at[dz], c_send.at[dz], c_recv.at[dz], other)
    ready = set()

    def pair_sum(dz):
        if dz not in ready:
            ready.add(dz)
            swaps[dz].wait_recv()
            for k in range(NXH):
                pair[dz, k] = core_in[dz, k].astype(F32) + prefix[meta_s[3, tile_row(dz, k, c)]]

    pl.semaphore_wait(x_near, 1)
    rings = {}

    def ring(k, slot):
        ahead, hop, needs = RINGS[k][slot]
        pair_sum(ahead % NZ)
        total = pair[ahead % NZ, k]
        for need in needs:
            rings[k, need].wait_recv()
            total = total + z_in[k, need].astype(F32)
        z_out[k, slot] = total.astype(BF)
        over = X_OFF[k] if slot in LAST else 0
        to = device(x=wrap(xh + over, NXH) * NXL + xl, z=wrap(z + hop, NZ))
        rings[k, slot] = send(z_out.at[k, slot], z_in.at[k, slot], z_send.at[k, slot], z_recv.at[k, slot], to)

    for turn, order in enumerate(RING_ORDER):
        for k, slot in order:
            ring(k, slot)
        if turn == 0:
            pair_sum(0)
            hops = []
            for k in range(NXH - 1):
                x_out[k] = pair[0, k].astype(BF)
                to = device(x=wrap(xh + X_OFF[k], NXH) * NXL + xl)
                hops.append(send(x_out.at[k], x_in.at[k], x_send.at[k], x_recv.at[k], to))
    total = pair[0, NXH - 1]
    for k, copy in enumerate(hops):
        copy.wait_recv()
        total = total + x_in[k].astype(F32)
    for order in RING_ORDER:
        for k, slot in order:
            if slot in LAST:
                rings[k, slot].wait_recv()
                total = total + z_in[k, slot].astype(F32)
    sent += list(swaps.values()) + list(rings.values()) + hops

    aggregated = total.astype(BF)
    pre = jnp.dot(aggregated, weight_ref[...], preferred_element_type=F32)
    sigmoid_pre = jax.nn.sigmoid(pre)
    out_ref[...] = (pre * sigmoid_pre).astype(BF)
    derivative = sigmoid_pre * (1.0 + pre * (1.0 - sigmoid_pre))
    grad_pre = (cot_ref[...].astype(F32) * derivative).astype(BF)
    part[...] = lax.dot_general(aggregated, grad_pre, (((0,), (0,)), ((), ())), preferred_element_type=F32)

    mine = pl.ds(pl.multiple_of(c * (S // 2), S // 2), S // 2)
    theirs = pl.ds(pl.multiple_of((1 - c) * (S // 2), S // 2), S // 2)
    swap = send(part.at[theirs], half_in, e_send.at[0], e_recv.at[0], other)
    swap.wait_recv()
    half[...] = part[mine] + half_in[...]
    sent.append(swap)
    axes = (
        (z, lambda k: device(z=wrap(z + k, NZ))),
        (x, lambda k: device(x=wrap(x + k, NX))),
        (y, lambda k: device(y=wrap(y + k, NY))),
    )
    for stage in range(3):
        copies = []
        for p, (start, size) in enumerate(PIECES):
            stage_out[stage, pl.ds(start, size)] = half[pl.ds(start, size)]
        for k in FAR_FIRST:
            for p, (start, size) in enumerate(PIECES):
                place_on, to = axes[(stage + p) % 3]
                rows = pl.ds(start, size)
                copies.append(send(
                    stage_out.at[stage, rows], stage_in.at[stage, place_on, rows],
                    w_send.at[stage, p, k], w_recv.at[stage, p, k], to(k),
                ))
        for p, (start, size) in enumerate(PIECES):
            rows = pl.ds(start, size)
            stage_in[stage, axes[(stage + p) % 3][0], rows] = half[rows]
        for copy in sent:
            copy.wait_send()
        for copy in copies:
            copy.wait_recv()
        total = stage_in[stage, 0]
        for n in range(1, 8):
            total = total + stage_in[stage, n]
        half[...] = total
        sent = copies
    swap = send(half, full_in, e_send.at[1], e_recv.at[1], other)
    grad_ref[mine] = half[...]
    for copy in sent:
        copy.wait_send()
    swap.wait()
    grad_ref[theirs] = full_in[...]


def on_device(features, tile_row, tile_col, tile_count, tile_vals, weight, cotangent):
    vmem = pl.BlockSpec(memory_space=pltpu.VMEM)
    dma = pltpu.SemaphoreType.DMA
    return pl.pallas_call(
        kernel,
        out_shape=(jax.ShapeDtypeStruct((S, S), BF), jax.ShapeDtypeStruct((S, S), F32)),
        in_specs=[pl.BlockSpec(memory_space=pltpu.SMEM)] + [pl.BlockSpec(memory_space=pltpu.HBM)] * 6,
        out_specs=(vmem, vmem),
        scratch_shapes=[
            pltpu.VMEM((S, S), BF),
            pltpu.VMEM((1, 1, SLOTS), I32),
            pltpu.VMEM((1, 1, SLOTS), I32),
            pltpu.VMEM((S, S), BF),
            pltpu.VMEM((S, S), BF),
            pltpu.VMEM((SLOTS, S, S), BF),
            pltpu.VMEM((COLS, S, S), BF),
            pltpu.VMEM((SLOTS + 1, S, S), F32),
            pltpu.VMEM((8, S), I32),
            pltpu.SMEM((8, S), I32),
            pltpu.VMEM((NZ, NXH, S, S), BF),
            pltpu.VMEM((NZ, NXH, S, S), BF),
            pltpu.VMEM((NZ, NXH, S, S), F32),
            pltpu.VMEM((NXH, 7, S, S), BF),
            pltpu.VMEM((NXH, 7, S, S), BF),
            pltpu.VMEM((3, S, S), BF),
            pltpu.VMEM((3, S, S), BF),
            pltpu.VMEM((S, S), F32),
            pltpu.VMEM((S // 2, S), F32),
            pltpu.VMEM((S // 2, S), F32),
            pltpu.VMEM((3, S // 2, S), F32),
            pltpu.VMEM((3, 8, S // 2, S), F32),
            pltpu.VMEM((S // 2, S), F32),
            dma((6,)), dma,
            dma((17,)), dma((17,)),
            dma((NZ,)), dma((NZ,)),
            dma((NXH, 7)), dma((NXH, 7)),
            dma((3,)), dma((3,)), pltpu.SemaphoreType.REGULAR,
            dma((3, 3, 8)), dma((3, 3, 8)),
            dma((2,)), dma((2,)),
        ],
        compiler_params=pltpu.CompilerParams(
            collective_id=0, has_side_effects=True, vmem_limit_bytes=40 * 2**20
        ),
    )(tile_count, *(
        pltpu.with_memory_space_constraint(value, pltpu.HBM)
        for value in (features, tile_row, tile_col, tile_vals, weight, cotangent)
    ))


def solution(mesh):
    return jax.shard_map(
        on_device,
        mesh=mesh,
        in_specs=(
            P(("col", "row"), None),
            P("row", "col", None),
            P("row", "col", None),
            P("row", "col"),
            P("row", "col", None, None, None),
            P(),
            P(("row", "col"), None),
        ),
        out_specs=(P(("row", "col"), None), P()),
        check_vma=False,
    )
```
